256 devices in a mesh: blk: 8 (over y, z_hi), uly: 32 (over z_lo, x, core).
Axes of the slice: x: 4, y: 4, z: 8 (z_hi: 2, z_lo: 4; z = z_hi * 4 + z_lo), core: 2. Of those that a mesh axis runs over, the one named last changes fastest.
Arguments:
- queries: bfloat16 [32768, 4096], P(('blk', 'uly')), may hold values from -64 to 64
- keys: bfloat16 [32768, 512], P(('blk', 'uly')), may hold values from -64 to 64
- values: bfloat16 [32768, 512], P(('blk', 'uly')), may hold values from -6 to 6
- output_gradient: bfloat16 [32768, 4096], P(('blk', 'uly')), may hold values from -6 to 6
- lengths: int32 [64], replicated, may hold values from 512 to 4096, as said below
Outputs:
- attended: bfloat16 [32768, 4096], P(('blk', 'uly'))
- query_grad: bfloat16 [32768, 4096], P(('blk', 'uly'))
- key_grad: bfloat16 [32768, 512], P(('blk', 'uly'))
- value_grad: bfloat16 [32768, 512], P(('blk', 'uly'))
The draws below stay inside these ranges and needn't reach their ends.
Inputs may be any that keep to these rules, and one draw needn't show every extreme that they name: `lengths`: documents are packed from token 0 in list order; the last one that begins before 32768 may run past the end and is cut there.
All inputs are finite; a program needn't handle non-finite values.
Results may differ from the reference program's by a relative error of at most 0.012.
Values may be sent and summed in bfloat16 or wider, within the bound.
A program may use at most 128 MiB of HBM per device.

```python
import math
import jax
import jax.numpy as jnp
from jax import lax

QUERY_HEADS = 32
KEY_VALUE_HEADS = 4
HEAD_SIZE = 128
PACKED_TOKENS = 32768
MAX_DOC = 4096
MIN_DOC = 512
QUERY_HEADS_RUN = 1


def draw_queries(key, part):
    key = jax.random.fold_in(key, 7)
    unmodified = jnp.clip(jax.random.normal(key, (PACKED_TOKENS, QUERY_HEADS * HEAD_SIZE), jnp.float32), -6.0, 6.0)
    return unmodified.astype(jnp.bfloat16)


def draw_keys(key, part):
    key = jax.random.fold_in(key, 9)
    unmodified = jnp.clip(jax.random.normal(key, (PACKED_TOKENS, KEY_VALUE_HEADS * HEAD_SIZE), jnp.float32), -6.0, 6.0)
    return unmodified.astype(jnp.bfloat16)


def draw_lengths(key, part):
    key = jax.random.fold_in(key, 5)
    first_key, second_key = jax.random.split(key)
    count = PACKED_TOKENS // MIN_DOC
    sizes = jax.random.randint(first_key, (count,), MIN_DOC, MAX_DOC + 1)
    spot = jax.random.randint(second_key, (), 0, PACKED_TOKENS // MAX_DOC)
    sizes = jnp.where(jnp.arange(count) == spot, MAX_DOC, sizes)
    return sizes.astype(jnp.int32)


def level_of(own_key, extent, cuts, least, top_value):
    def one(position, parts):
        steps = jax.random.uniform(jax.random.fold_in(jax.random.fold_in(own_key, 6), position), (parts,), jnp.float32, least / len(cuts), top_value / len(cuts))
        return jnp.repeat(jnp.exp(steps), extent[position] // parts).reshape((-1,) + (1,) * (len(extent) - position - 1))

    gain = one(*cuts[0])
    for cut in cuts[1:]:
        gain = gain * one(*cut)
    return gain


def centred(stream_key, shape, width, most, shards=(), kind=jnp.bfloat16):
    array = jax.random.normal(stream_key, shape, jnp.float32) * width
    if len(shards) > 0:
        array = level_of(stream_key, shape, shards, -0.22, 0.18) * array
    return jnp.clip(array, min=-most, max=most).astype(kind)


def setup_inputs(seed: int = 0) -> dict:
    streams_of = jax.random.split(jax.random.key(seed), 6)
    return {
        "queries": draw_queries(jax.random.fold_in(streams_of[5], 71), 0),
        "keys": draw_keys(jax.random.fold_in(streams_of[5], 71), 0),
        "values": centred(streams_of[2], (PACKED_TOKENS, KEY_VALUE_HEADS * HEAD_SIZE), 1.0, 6.0, ((0, 256),)),
        "output_gradient": centred(streams_of[3], (PACKED_TOKENS, QUERY_HEADS * HEAD_SIZE), 1.0, 6.0, ((0, 256),)),
        "lengths": draw_lengths(jax.random.fold_in(streams_of[5], 71), 0),
    }


NEGATIVE_FILL = -1e+30

def doc_numbers(positions, doc_ends):
    counted = lax.optimization_barrier(jnp.sum((doc_ends[None, :] <= positions[:, None]).astype(jnp.int32), axis=1))
    return jnp.where(positions < 0, -1, counted).astype(jnp.int32)

def reference(queries, keys, values, output_gradient, lengths):
    score_scale = 1.0 / math.sqrt(HEAD_SIZE)
    queries_per_key = QUERY_HEADS // KEY_VALUE_HEADS
    run_total_count = queries_per_key // QUERY_HEADS_RUN
    query_row_block = min(512, MAX_DOC)
    key_row_block = min(128, MAX_DOC)
    doc_ends = jnp.cumsum(lengths).astype(jnp.int32)
    doc_starts = (doc_ends - lengths).astype(jnp.int32)
    positions = jnp.arange(PACKED_TOKENS).astype(jnp.int32)
    doc_ids = doc_numbers(positions, doc_ends)
    query_gathered = queries.reshape(PACKED_TOKENS, KEY_VALUE_HEADS, queries_per_key, HEAD_SIZE)
    gradient_gathered = output_gradient.reshape(PACKED_TOKENS, KEY_VALUE_HEADS, queries_per_key, HEAD_SIZE)
    key_gathered = keys.reshape(PACKED_TOKENS, KEY_VALUE_HEADS, HEAD_SIZE)
    value_gathered = values.reshape(PACKED_TOKENS, KEY_VALUE_HEADS, HEAD_SIZE)

    def tile_scores(query_block, block_docs, block_positions, tile_index):
        first_key = (tile_index * key_row_block).astype(jnp.int32)
        key_tile = lax.dynamic_slice_in_dim(key_gathered, first_key, key_row_block, 0).astype(jnp.float32)
        value_tile = lax.dynamic_slice_in_dim(value_gathered, first_key, key_row_block, 0).astype(jnp.float32)
        tile_docs = lax.dynamic_slice_in_dim(doc_ids, first_key, key_row_block, 0)
        tile_positions = lax.dynamic_slice_in_dim(positions, first_key, key_row_block, 0)
        scores = jnp.einsum('qagd,kad->agqk', query_block, key_tile) * score_scale
        allowed = (block_docs[:, None] == tile_docs[None, :]) & (tile_positions[None, :] <= block_positions[:, None])
        return (scores, allowed[None, None], key_tile, value_tile, first_key)

    def one_block(block_index, carried):
        out_rows, query_grads, key_runs, value_runs = carried
        first_row = (block_index * query_row_block).astype(jnp.int32)
        query_block = lax.dynamic_slice_in_dim(query_gathered, first_row, query_row_block, 0).astype(jnp.float32)
        grad_block = lax.dynamic_slice_in_dim(gradient_gathered, first_row, query_row_block, 0).astype(jnp.float32)
        block_docs = lax.dynamic_slice_in_dim(doc_ids, first_row, query_row_block, 0)
        block_positions = lax.dynamic_slice_in_dim(positions, first_row, query_row_block, 0)
        lead = doc_starts[block_docs[0]]
        tile_lower = (lead // key_row_block).astype(jnp.int32)
        tile_upper = ((first_row + query_row_block) // key_row_block).astype(jnp.int32)

        def first_pass(tile_index, running):
            row_max, row_sum = running
            scores, allowed, key_tile, value_tile, first_key = tile_scores(query_block, block_docs, block_positions, tile_index)
            new_max = jnp.maximum(row_max, lax.optimization_barrier(jnp.max(jnp.where(allowed, scores, NEGATIVE_FILL), axis=3)))
            kept = jnp.where(allowed, jnp.exp(scores - new_max[..., None]), 0.0)
            return (new_max, row_sum * jnp.exp(row_max - new_max) + lax.optimization_barrier(jnp.sum(kept, axis=3)))
        initial_maximum = jnp.full((KEY_VALUE_HEADS, queries_per_key, query_row_block), NEGATIVE_FILL, jnp.float32)
        initial_total = jnp.zeros((KEY_VALUE_HEADS, queries_per_key, query_row_block), jnp.float32)
        row_max, row_sum = lax.fori_loop(tile_lower, tile_upper, first_pass, (initial_maximum, initial_total))
        log_total = row_max + jnp.log(row_sum)

        def later_sweep(tile_index, weighted_values):
            scores, allowed, key_tile, value_tile, first_key = tile_scores(query_block, block_docs, block_positions, tile_index)
            probability = jnp.where(allowed, jnp.exp(scores - log_total[..., None]), 0.0)
            probs_low = lax.optimization_barrier(probability.astype(jnp.bfloat16)).astype(jnp.float32)
            return weighted_values + jnp.einsum('agqk,kad->qagd', probs_low, value_tile)
        weighted_values = lax.fori_loop(tile_lower, tile_upper, later_sweep, jnp.zeros((query_row_block, KEY_VALUE_HEADS, queries_per_key, HEAD_SIZE), jnp.float32))
        out_block = weighted_values.astype(jnp.bfloat16)
        out_wide = lax.optimization_barrier(out_block).astype(jnp.float32)
        row_dot = jnp.transpose(lax.optimization_barrier(jnp.sum(grad_block * out_wide, axis=3)), (1, 2, 0))

        def third_pass(tile_index, sums):
            query_step, key_inner, value_inner = sums
            scores, allowed, key_tile, value_tile, first_key = tile_scores(query_block, block_docs, block_positions, tile_index)
            probability = jnp.where(allowed, jnp.exp(scores - log_total[..., None]), 0.0)
            probs_low = lax.optimization_barrier(probability.astype(jnp.bfloat16)).astype(jnp.float32)
            grad_probs = jnp.einsum('qagd,kad->agqk', grad_block, value_tile)
            dscore = probability * (grad_probs - row_dot[..., None]) * score_scale
            dscore = lax.optimization_barrier(dscore.astype(jnp.bfloat16)).astype(jnp.float32)
            query_step = query_step + jnp.einsum('agqk,kad->qagd', dscore, key_tile)
            key_advance = jnp.einsum('agqk,qagd->kagd', dscore, query_block)
            value_advance = jnp.einsum('agqk,qagd->kagd', probs_low, grad_block)
            key_advance = lax.optimization_barrier(jnp.sum(key_advance.reshape(key_row_block, KEY_VALUE_HEADS, run_total_count, QUERY_HEADS_RUN, HEAD_SIZE), axis=3))
            value_advance = lax.optimization_barrier(jnp.sum(value_advance.reshape(key_row_block, KEY_VALUE_HEADS, run_total_count, QUERY_HEADS_RUN, HEAD_SIZE), axis=3))
            key_inner = lax.dynamic_update_slice_in_dim(key_inner, lax.dynamic_slice_in_dim(key_inner, first_key, key_row_block, 0) + key_advance, first_key, 0)
            value_inner = lax.dynamic_update_slice_in_dim(value_inner, lax.dynamic_slice_in_dim(value_inner, first_key, key_row_block, 0) + value_advance, first_key, 0)
            return (query_step, key_inner, value_inner)
        initial_gradient = jnp.zeros((query_row_block, KEY_VALUE_HEADS, queries_per_key, HEAD_SIZE), jnp.float32)
        query_step, key_runs, value_runs = lax.fori_loop(tile_lower, tile_upper, third_pass, (initial_gradient, key_runs, value_runs))
        out_rows = lax.dynamic_update_slice_in_dim(out_rows, out_block, first_row, 0)
        query_grads = lax.dynamic_update_slice_in_dim(query_grads, query_step.astype(jnp.bfloat16), first_row, 0)
        return (out_rows, query_grads, key_runs, value_runs)
    initial = (jnp.zeros((PACKED_TOKENS, KEY_VALUE_HEADS, queries_per_key, HEAD_SIZE), jnp.bfloat16), jnp.zeros((PACKED_TOKENS, KEY_VALUE_HEADS, queries_per_key, HEAD_SIZE), jnp.bfloat16), jnp.zeros((PACKED_TOKENS, KEY_VALUE_HEADS, run_total_count, HEAD_SIZE), jnp.float32), jnp.zeros((PACKED_TOKENS, KEY_VALUE_HEADS, run_total_count, HEAD_SIZE), jnp.float32))
    out_rows, query_grads, key_runs, value_runs = lax.fori_loop(0, PACKED_TOKENS // query_row_block, one_block, initial)

    def fold_runs(run_partial_sums):
        return lax.optimization_barrier(jnp.sum(run_partial_sums, axis=2)).astype(jnp.bfloat16).reshape(PACKED_TOKENS, KEY_VALUE_HEADS * HEAD_SIZE)
    return (out_rows.reshape(PACKED_TOKENS, QUERY_HEADS * HEAD_SIZE), query_grads.reshape(PACKED_TOKENS, QUERY_HEADS * HEAD_SIZE), fold_runs(key_runs), fold_runs(value_runs))
```

```python
import math

import jax
import jax.numpy as jnp
from jax import lax
from jax.experimental import pallas as pl
from jax.experimental.pallas import tpu as pltpu
from jax.sharding import Mesh, PartitionSpec as P

HEAD = 128
KEY_VALUE_HEADS = 4
MAX_DOC = 4096

SCALE = 1.0 / math.sqrt(HEAD)
SCALE_LOG2 = SCALE * math.log2(math.e)
NEGATIVE_FILL = -1e30

Z_LOW, X_SIZE, CORES = 4, 4, 2
RING = X_SIZE * CORES
REACH = 4
TOKENS = 128
STEP_ROWS = TOKENS * RING
WINDOW = (REACH + 1) * STEP_ROWS
HEADS = 4
WIDTH = HEADS * HEAD

BLOCK = 512
TILE = 512

MESH = pl.DeviceIdType.MESH
ANY = pl.BlockSpec(memory_space=pl.ANY)
VMEM = pl.BlockSpec(memory_space=pltpu.VMEM)
SMEM = pl.BlockSpec(memory_space=pltpu.SMEM)


def dot(a, b):
    return jnp.dot(a, b, preferred_element_type=jnp.float32)


def place():
    blk, zl = lax.axis_index("blk"), lax.axis_index("zl")
    x, core = lax.axis_index("x"), lax.axis_index("core")
    me = x * CORES + core
    steps = lax.axis_size("blk") * Z_LOW

    def ring(by):
        peer = (me + by + RING) % RING
        return peer, (blk, zl, peer // CORES, peer % CORES)

    def along(by):
        step = (blk * Z_LOW + zl + by + steps) % steps
        return (step // Z_LOW, step % Z_LOW, x, core)

    def across(by):
        peer = (x + by + X_SIZE) % X_SIZE
        return peer, (blk, zl, peer, core)

    return me, x, core, ring, along, across


def greet(ring, along):
    barrier = pltpu.get_barrier_semaphore()
    for by in range(1, RING):
        pl.semaphore_signal(barrier, inc=1, device_id=ring(by)[1], device_id_type=MESH)
    for by in (1, -1):
        pl.semaphore_signal(barrier, inc=1, device_id=along(by), device_id_type=MESH)
    pl.semaphore_wait(barrier, RING + 1)


def remote(src, dst, send, recv, device):
    return pltpu.make_async_remote_copy(
        src_ref=src, dst_ref=dst, send_sem=send, recv_sem=recv, device_id=device, device_id_type=MESH
    )


def gather_kernel(
    queries, grads, keys, values, query_rows, grad_rows, window,
    own_sem, row_send, row_recv, head_send, head_recv, hop_send, hop_recv, pair_send, pair_recv,
):
    me, x, core, ring, along, across = place()
    greet(ring, along)

    def head_columns(head):
        return pl.ds(pl.multiple_of(head * HEAD, HEAD), HEAD)

    def row_columns(peer):
        return pl.ds(pl.multiple_of(peer * WIDTH, WIDTH), WIDTH)

    def token_rows(peer):
        return pl.ds(pl.multiple_of(peer * TOKENS, TOKENS), TOKENS)

    pending = []
    for i, source in enumerate((keys, values)):
        for by in range(1, X_SIZE):
            peer, device = across(by)
            copy = remote(
                source.at[:, head_columns(peer)], window.at[i, REACH, x, core],
                head_send.at[i, by], head_recv.at[i, by], device,
            )
            copy.start()
            pending.append(copy)
    own = []
    for i, source in enumerate((keys, values)):
        own.append(
            pltpu.make_async_copy(
                source.at[:, head_columns(x)], window.at[i, REACH, x, core], own_sem.at[i]
            )
        )
        own[-1].start()

    def send_rows(i, source, target):
        for by in range(1, RING):
            peer, device = ring(by)
            copy = remote(
                source.at[:, row_columns(peer)], target.at[token_rows(me), :],
                row_send.at[i, by], row_recv.at[i, by], device,
            )
            copy.start()
            pending.append(copy)
        own.append(
            pltpu.make_async_copy(
                source.at[:, row_columns(me)], target.at[token_rows(me), :], own_sem.at[2 + i]
            )
        )
        own[-1].start()

    send_rows(0, queries, query_rows)

    _, pair = ring(1 - 2 * core)
    for hop in range(REACH + 1):
        at = REACH - hop
        for i in range(2):
            half = window.at[i, at, :, core]
            if hop == 0:
                own[i].wait()
                for by in range(1, X_SIZE):
                    peer, device = across(-by)
                    remote(
                        keys.at[:, head_columns(x)], window.at[i, REACH, peer, core],
                        head_send.at[i, by], head_recv.at[i, by], device,
                    ).wait_recv()
            else:
                remote(
                    half, half, hop_send.at[i, hop - 1], hop_recv.at[i, hop - 1], along(-1)
                ).wait_recv()
            if hop < REACH:
                copy = remote(
                    half, window.at[i, at - 1, :, core], hop_send.at[i, hop], hop_recv.at[i, hop], along(1)
                )
                copy.start()
                pending.append(copy)
            copy = remote(half, half, pair_send.at[i, hop], pair_recv.at[i, hop], pair)
            copy.start()
            pending.append(copy)
        if hop == 0:
            send_rows(1, grads, grad_rows)

    for copy in own[2:]:
        copy.wait()
    for i, target in enumerate((query_rows, grad_rows)):
        for by in range(1, RING):
            peer, device = ring(-by)
            here = target.at[token_rows(peer), :]
            remote(here, here, row_send.at[i, by], row_recv.at[i, by], device).wait_recv()
    for hop in range(REACH + 1):
        for i in range(2):
            half = window.at[i, REACH - hop, :, 1 - core]
            remote(half, half, pair_send.at[i, hop], pair_recv.at[i, hop], pair).wait_recv()
    for copy in pending:
        copy.wait_send()


def gather(queries, grads, keys, values):
    rows = jax.ShapeDtypeStruct((STEP_ROWS, WIDTH), jnp.bfloat16)
    dma = pltpu.SemaphoreType.DMA
    return pl.pallas_call(
        gather_kernel,
        out_shape=(
            rows,
            rows,
            jax.ShapeDtypeStruct((2, REACH + 1, X_SIZE, CORES, TOKENS, HEAD), jnp.bfloat16),
        ),
        in_specs=[ANY] * 4,
        out_specs=(ANY,) * 3,
        scratch_shapes=[
            dma((4,)), dma((2, RING)), dma((2, RING)), dma((2, X_SIZE)), dma((2, X_SIZE)),
            dma((2, REACH)), dma((2, REACH)), dma((2, REACH + 1)), dma((2, REACH + 1)),
        ],
        compiler_params=pltpu.CompilerParams(collective_id=0, has_side_effects=True),
        name="gather_rows",
    )(queries, grads, keys, values)


def scatter_kernel(
    attended_rows, query_grad_rows, terms, attended, query_grad, key_grad, value_grad,
    pair_in, hop_in, outgoing, own_sem, row_send, row_recv, head_send, head_recv,
    hop_send, hop_recv, pair_send, pair_recv,
):
    me, x, core, ring, along, across = place()
    greet(ring, along)

    def head_columns(head):
        return pl.ds(pl.multiple_of(head * HEAD, HEAD), HEAD)

    def row_columns(peer):
        return pl.ds(pl.multiple_of(peer * WIDTH, WIDTH), WIDTH)

    def token_rows(peer):
        return pl.ds(pl.multiple_of(peer * TOKENS, TOKENS), TOKENS)

    pending, own = [], []
    _, pair = ring(1 - 2 * core)
    for at in range(REACH + 1):
        for i in range(2):
            copy = remote(
                terms.at[i, at, :, 1 - core], pair_in.at[i, at], pair_send.at[i, at], pair_recv.at[i, at], pair
            )
            copy.start()
            pending.append(copy)

    def send_rows(i, source, target):
        for by in range(1, RING):
            peer, device = ring(by)
            copy = remote(
                source.at[token_rows(peer), :], target.at[:, row_columns(me)],
                row_send.at[i, by], row_recv.at[i, by], device,
            )
            copy.start()
            pending.append(copy)
        own.append(
            pltpu.make_async_copy(
                source.at[token_rows(me), :], target.at[:, row_columns(me)], own_sem.at[i]
            )
        )
        own[-1].start()

    send_rows(0, attended_rows, attended)

    for at in range(REACH + 1):
        for i in range(2):
            pair_copy = remote(
                pair_in.at[i, at], pair_in.at[i, at], pair_send.at[i, at], pair_recv.at[i, at], pair
            )
            pair_copy.wait_recv()
            total = terms[i, at, :, core].astype(jnp.float32) + pair_in[i, at].astype(jnp.float32)
            if at > 0:
                remote(
                    hop_in.at[i, at - 1], hop_in.at[i, at - 1],
                    hop_send.at[i, at - 1], hop_recv.at[i, at - 1], along(1),
                ).wait_recv()
                total = total + hop_in[i, at - 1].astype(jnp.float32)
            outgoing[i, at] = total.astype(jnp.bfloat16)
            if at < REACH:
                copy = remote(
                    outgoing.at[i, at], hop_in.at[i, at], hop_send.at[i, at], hop_recv.at[i, at], along(-1)
                )
                copy.start()
                pending.append(copy)
                continue
            target = (key_grad, value_grad)[i]
            for by in range(1, X_SIZE):
                peer, device = across(by)
                copy = remote(
                    outgoing.at[i, REACH, peer], target.at[:, head_columns(x)],
                    head_send.at[i, by], head_recv.at[i, by], device,
                )
                copy.start()
                pending.append(copy)
            own.append(
                pltpu.make_async_copy(
                    outgoing.at[i, REACH, x], target.at[:, head_columns(x)], own_sem.at[2 + i]
                )
            )
            own[-1].start()
        if at == 0:
            send_rows(1, query_grad_rows, query_grad)

    for copy in own:
        copy.wait()
    for i, target in enumerate((attended, query_grad)):
        for by in range(1, RING):
            peer, device = ring(-by)
            here = target.at[:, row_columns(peer)]
            remote(here, here, row_send.at[i, by], row_recv.at[i, by], device).wait_recv()
    for i, target in enumerate((key_grad, value_grad)):
        for by in range(1, X_SIZE):
            peer, device = across(-by)
            here = target.at[:, head_columns(peer)]
            remote(here, here, head_send.at[i, by], head_recv.at[i, by], device).wait_recv()
    for copy in pending:
        copy.wait_send()


def scatter(attended_rows, query_grad_rows, terms):
    wide = jax.ShapeDtypeStruct((TOKENS, RING * WIDTH), jnp.bfloat16)
    narrow = jax.ShapeDtypeStruct((TOKENS, KEY_VALUE_HEADS * HEAD), jnp.bfloat16)
    dma = pltpu.SemaphoreType.DMA
    half = (X_SIZE, TOKENS, HEAD)
    return pl.pallas_call(
        scatter_kernel,
        out_shape=(wide, wide, narrow, narrow),
        in_specs=[ANY, ANY, VMEM],
        out_specs=(ANY,) * 4,
        scratch_shapes=[
            pltpu.VMEM((2, REACH + 1) + half, jnp.bfloat16),
            pltpu.VMEM((2, REACH) + half, jnp.bfloat16),
            pltpu.VMEM((2, REACH + 1) + half, jnp.bfloat16),
            dma((4,)), dma((2, RING)), dma((2, RING)), dma((2, X_SIZE)), dma((2, X_SIZE)),
            dma((2, REACH)), dma((2, REACH)), dma((2, REACH + 1)), dma((2, REACH + 1)),
        ],
        compiler_params=pltpu.CompilerParams(
            collective_id=1, has_side_effects=True, vmem_limit_bytes=40 * 2**20
        ),
        name="scatter_rows",
    )(attended_rows, query_grad_rows, terms)


def head_slice(head):
    return slice(head * HEAD, (head + 1) * HEAD)


def attention_kernel(
    lengths, queries, grads, window, attended, query_grad, terms,
    starts, edges, keys_t, values_t, queries_t, grads_t, scores_all, top_rows, sum_rows, acc, key_sums, value_sums,
):
    step = lax.axis_index("blk") * Z_LOW + lax.axis_index("zl")
    base = (step - REACH) * STEP_ROWS
    blocks = STEP_ROWS // BLOCK

    places = REACH * STEP_ROWS + lax.broadcasted_iota(jnp.int32, (1, STEP_ROWS), 1)
    ends = [REACH * STEP_ROWS + b * BLOCK + e for b in range(blocks) for e in (0, BLOCK - 1)]

    def next_document(i, carried):
        end, row, firsts = carried
        end = end + lengths[i]
        firsts = tuple(jnp.where(end <= at, end, one) for at, one in zip(ends, firsts))
        return end, jnp.where(end <= places, end, row), firsts

    origin = jnp.int32(0) - base
    _, row, firsts = lax.fori_loop(
        0,
        lengths.shape[0],
        next_document,
        (origin, jnp.full((1, STEP_ROWS), origin, jnp.int32), (origin,) * len(ends)),
    )
    starts[...] = row
    for n, one in enumerate(firsts):
        edges[n] = one

    for part in range(0, WINDOW, 512):
        here = slice(part, part + 512)
        keys_t[:, here] = window[0, here, :].T
        values_t[:, here] = window[1, here, :].T
    key_sums[...] = jnp.zeros_like(key_sums)
    value_sums[...] = jnp.zeros_like(value_sums)

    @pl.loop(0, blocks)
    def _(block):
        first_row = pl.multiple_of(block * BLOCK, BLOCK)
        rows = pl.ds(first_row, BLOCK)
        first = REACH * STEP_ROWS + first_row
        hi = (first + BLOCK + TILE - 1) // TILE
        full_hi = (first + 1) // TILE
        lo = jnp.maximum(edges[2 * block], 0) // TILE
        full_lo = jnp.minimum((jnp.maximum(edges[2 * block + 1], 0) + TILE - 1) // TILE, full_hi)
        for head in range(HEADS):
            queries_t[head] = queries[rows, head_slice(head)].T
            grads_t[head] = grads[rows, head_slice(head)].T
        top_rows[...] = jnp.full_like(top_rows, NEGATIVE_FILL)
        sum_rows[...] = jnp.zeros_like(sum_rows)
        acc[...] = jnp.zeros_like(acc)

        def score(tile, masked):
            first_key = pl.multiple_of(tile * TILE, TILE)
            key_tile = window[0, pl.ds(first_key, TILE), :]
            slot = pl.ds(pl.multiple_of((tile - lo) * TILE, TILE), TILE)
            if masked:
                key_at = first_key + lax.broadcasted_iota(jnp.int32, (TILE, BLOCK), 0)
                query_at = first + lax.broadcasted_iota(jnp.int32, (1, BLOCK), 1)
                allowed = (key_at >= starts[:, rows]) & (key_at <= query_at)
            for head in range(HEADS):
                scores = dot(key_tile, queries_t[head])
                if masked:
                    scores = jnp.where(allowed, scores, NEGATIVE_FILL)
                scores_all[head, slot, :] = scores
                top_rows[head] = jnp.maximum(
                    top_rows[head], jnp.max(scores.reshape(TILE // 8, 8, BLOCK), axis=0)
                )

        pl.loop(lo, full_lo)(lambda tile: score(tile, True))
        pl.loop(full_lo, full_hi)(lambda tile: score(tile, False))
        pl.loop(full_hi, hi)(lambda tile: score(tile, True))
        top = [jnp.max(top_rows[head], axis=0, keepdims=True) for head in range(HEADS)]

        def attend(tile):
            value_tile_t = values_t[:, pl.ds(pl.multiple_of(tile * TILE, TILE), TILE)]
            slot = pl.ds(pl.multiple_of((tile - lo) * TILE, TILE), TILE)
            for head in range(HEADS):
                kept = jnp.exp2((scores_all[head, slot, :] - top[head]) * SCALE_LOG2)
                sum_rows[head] += jnp.sum(kept.reshape(TILE // 8, 8, BLOCK), axis=0)
                acc[head] += dot(value_tile_t, kept.astype(jnp.bfloat16))

        pl.loop(lo, hi)(attend)
        row_dot, log_total = [], []
        for head in range(HEADS):
            total = jnp.sum(sum_rows[head], axis=0, keepdims=True)
            out_t = (acc[head] / total).astype(jnp.bfloat16)
            attended[rows, head_slice(head)] = out_t.T
            row_dot.append(
                jnp.sum(
                    grads_t[head].astype(jnp.float32) * out_t.astype(jnp.float32), axis=0, keepdims=True
                )
            )
            log_total.append(top[head] * SCALE_LOG2 + jnp.log2(total))
        acc[...] = jnp.zeros_like(acc)

        def grad(tile):
            here = pl.ds(pl.multiple_of(tile * TILE, TILE), TILE)
            slot = pl.ds(pl.multiple_of((tile - lo) * TILE, TILE), TILE)
            value_tile = window[1, here, :]
            key_tile_t = keys_t[:, here]
            key_sum = key_sums[here, :]
            value_sum = value_sums[here, :]
            for head in range(HEADS):
                probability = jnp.exp2(scores_all[head, slot, :] * SCALE_LOG2 - log_total[head])
                grad_probs = dot(value_tile, grads_t[head])
                dscore = (probability * (grad_probs - row_dot[head])).astype(jnp.bfloat16)
                value_sum = value_sum + dot(
                    probability.astype(jnp.bfloat16), grads[rows, head_slice(head)]
                )
                key_sum = key_sum + dot(dscore, queries[rows, head_slice(head)])
                acc[head] += dot(key_tile_t, dscore)
            key_sums[here, :] = key_sum
            value_sums[here, :] = value_sum

        pl.loop(lo, hi)(grad)
        for head in range(HEADS):
            query_grad[rows, head_slice(head)] = (acc[head] * SCALE).T.astype(jnp.bfloat16)

    terms[0] = (key_sums[...] * SCALE).astype(jnp.bfloat16)
    terms[1] = value_sums[...].astype(jnp.bfloat16)


def attention(lengths, queries, grads, window):
    rows = jax.ShapeDtypeStruct((STEP_ROWS, WIDTH), jnp.bfloat16)
    pairs = HEADS * STEP_ROWS * WINDOW // 2
    return pl.pallas_call(
        attention_kernel,
        out_shape=(rows, rows, jax.ShapeDtypeStruct((2, WINDOW, HEAD), jnp.bfloat16)),
        in_specs=[SMEM, VMEM, VMEM, VMEM],
        out_specs=(VMEM,) * 3,
        scratch_shapes=[
            pltpu.VMEM((1, STEP_ROWS), jnp.int32),
            pltpu.SMEM((2 * STEP_ROWS // BLOCK,), jnp.int32),
            pltpu.VMEM((HEAD, WINDOW), jnp.bfloat16),
            pltpu.VMEM((HEAD, WINDOW), jnp.bfloat16),
            pltpu.VMEM((HEADS, HEAD, BLOCK), jnp.bfloat16),
            pltpu.VMEM((HEADS, HEAD, BLOCK), jnp.bfloat16),
            pltpu.VMEM((HEADS, MAX_DOC + BLOCK, BLOCK), jnp.float32),
            pltpu.VMEM((HEADS, 8, BLOCK), jnp.float32),
            pltpu.VMEM((HEADS, 8, BLOCK), jnp.float32),
            pltpu.VMEM((HEADS, HEAD, BLOCK), jnp.float32),
            pltpu.VMEM((WINDOW, HEAD), jnp.float32),
            pltpu.VMEM((WINDOW, HEAD), jnp.float32),
        ],
        compiler_params=pltpu.CompilerParams(vmem_limit_bytes=63 * 2**20),
        cost_estimate=pl.CostEstimate(
            flops=14 * HEAD * pairs, bytes_accessed=10 * 2**20, transcendentals=2 * pairs
        ),
        name="attention",
    )(lengths, queries, grads, window)


def shards(queries, keys, values, output_gradient, lengths):
    query_rows, grad_rows, window = gather(queries, output_gradient, keys, values)
    attended_rows, query_grad_rows, terms = attention(
        lengths, query_rows, grad_rows, window.reshape(2, WINDOW, HEAD)
    )
    return scatter(
        attended_rows,
        query_grad_rows,
        terms.reshape(2, REACH + 1, X_SIZE, CORES, TOKENS, HEAD),
    )


def solution(mesh):
    wide = Mesh(
        mesh.devices.reshape(-1, Z_LOW, X_SIZE, CORES),
        ("blk", "zl", "x", "core"),
    )
    spec = P(("blk", "zl", "x", "core"), None)
    return jax.shard_map(
        shards,
        mesh=wide,
        in_specs=(spec, spec, spec, spec, P()),
        out_specs=(spec, spec, spec, spec),
        check_vma=False,
    )
```

```python
import math

import jax
import jax.numpy as jnp
from jax import lax
from jax.experimental import pallas as pl
from jax.experimental.pallas import tpu as pltpu
from jax.sharding import Mesh, PartitionSpec as P

HEAD = 128
KEY_VALUE_HEADS = 4

SCALE = 1.0 / math.sqrt(HEAD)
SCALE_LOG2 = SCALE * math.log2(math.e)
NEGATIVE_FILL = -1e30

Z_LOW, X_SIZE, CORES = 4, 4, 2
RING = X_SIZE * CORES
REACH = 4
TOKENS = 128
STEP_ROWS = TOKENS * RING
HEADS = 4
WIDTH = HEADS * HEAD

BLOCK = 512
BLOCKS = STEP_ROWS // BLOCK
PARTS = BLOCK // (CORES * TOKENS)
TILES = BLOCKS * REACH + 1

MESH = pl.DeviceIdType.MESH
ANY = pl.BlockSpec(memory_space=pl.ANY)
SMEM = pl.BlockSpec(memory_space=pltpu.SMEM)


def dot(a, b):
    return jnp.dot(a, b, preferred_element_type=jnp.float32)


def place():
    blk, zl = lax.axis_index("blk"), lax.axis_index("zl")
    x, core = lax.axis_index("x"), lax.axis_index("core")
    steps = lax.axis_size("blk") * Z_LOW

    def ring(by):
        peer = (x * CORES + core + by + RING) % RING
        return peer, (blk, zl, peer // CORES, peer % CORES)

    def along(by):
        step = (blk * Z_LOW + zl + by + steps) % steps
        return (step // Z_LOW, step % Z_LOW, x, core)

    def across(by):
        peer = (x + by + X_SIZE) % X_SIZE
        return peer, (blk, zl, peer, core)

    return blk * Z_LOW + zl, x * CORES + core, x, core, ring, along, across


def remote(src, dst, send, recv, device):
    return pltpu.make_async_remote_copy(
        src_ref=src, dst_ref=dst, send_sem=send, recv_sem=recv, device_id=device, device_id_type=MESH
    )


def head_columns(head):
    return pl.ds(pl.multiple_of(head * HEAD, HEAD), HEAD)


def row_columns(peer):
    return pl.ds(pl.multiple_of(peer * WIDTH, WIDTH), WIDTH)


def token_rows(peer):
    return pl.ds(pl.multiple_of(peer * TOKENS, TOKENS), TOKENS)


def block_rows(block):
    return slice(block * BLOCK, (block + 1) * BLOCK)


def tiles_of(distance, block):
    if distance == 0:
        return [(tile, tile) for tile in range(block + 1)]
    base = block + 1 + (distance - 1) * BLOCKS
    if distance == REACH:
        return [(tile, base + tile - block) for tile in range(block, BLOCKS)]
    return [(tile, base + tile) for tile in range(BLOCKS)]


def kernel(
    lengths, queries, grads, keys, values,
    attended, query_grad, key_grad, value_grad,
    window, query_rows, grad_rows, queries_t, grads_t, chunk_t, starts, scores, probs, tops, top, total, row_dot,
    acc, out_rows, chunk_sums, kept_sums, pair_out, pair_in, hop_in, outgoing,
    own_sem, row_send, row_recv, head_send, head_recv, hop_send, hop_recv, pair_send, pair_recv,
    out_own, out_send, out_recv, sum_own, sum_send, sum_recv, back_send, back_recv, swap_send, swap_recv,
):
    step, me, x, core, ring, along, across = place()
    _, pair = ring(1 - 2 * core)

    barrier = pltpu.get_barrier_semaphore()
    for by in range(1, RING):
        pl.semaphore_signal(barrier, inc=1, device_id=ring(by)[1], device_id_type=MESH)
    for by in (1, -1):
        pl.semaphore_signal(barrier, inc=1, device_id=along(by), device_id_type=MESH)
    pl.semaphore_wait(barrier, RING + 1)

    pending = []

    def send(copy):
        copy.start()
        pending.append(copy)

    for i, source in enumerate((keys, values)):
        for by in range(1, X_SIZE):
            peer, device = across(by)
            send(
                remote(
                    source.at[:, head_columns(peer)], window.at[i, REACH, x, core],
                    head_send.at[i, by], head_recv.at[i, by], device,
                )
            )
    own = [
        pltpu.make_async_copy(source.at[:, head_columns(x)], window.at[i, REACH, x, core], own_sem.at[i])
        for i, source in enumerate((keys, values))
    ]
    own += [
        pltpu.make_async_copy(source.at[:, row_columns(me)], target.at[token_rows(me), :], own_sem.at[2 + i])
        for i, (source, target) in enumerate(((queries, query_rows), (grads, grad_rows)))
    ]
    for copy in own:
        copy.start()

    def send_rows(i, source, target):
        for by in range(1, RING):
            peer, device = ring(by)
            send(
                remote(
                    source.at[:, row_columns(peer)], target.at[token_rows(me), :],
                    row_send.at[i, by], row_recv.at[i, by], device,
                )
            )

    def await_rows(i, target):
        own[2 + i].wait()
        for by in range(1, RING):
            peer, device = ring(-by)
            here = target.at[token_rows(peer), :]
            remote(here, here, row_send.at[i, by], row_recv.at[i, by], device).wait_recv()

    send_rows(0, queries, query_rows)

    base = (step - REACH) * STEP_ROWS
    places = REACH * STEP_ROWS + lax.broadcasted_iota(jnp.int32, (1, STEP_ROWS), 1)

    def next_document(i, carried):
        end, row = carried
        end = end + lengths[i]
        return end, jnp.where(end <= places, end, row)

    _, row = lax.fori_loop(
        0, lengths.shape[0], next_document, (-base, jnp.zeros((1, STEP_ROWS), jnp.int32) - base)
    )
    starts[...] = row
    top[...] = jnp.full_like(top, NEGATIVE_FILL)
    total[...] = jnp.zeros_like(total)
    acc[...] = jnp.zeros_like(acc)

    def pass_on(distance):
        at = REACH - distance
        for i in range(2):
            half = window.at[i, at, :, core]
            if distance == 0:
                own[i].wait()
                for by in range(1, X_SIZE):
                    peer, device = across(-by)
                    here = window.at[i, REACH, peer, core]
                    remote(here, here, head_send.at[i, by], head_recv.at[i, by], device).wait_recv()
            else:
                remote(
                    half, half, hop_send.at[i, distance - 1], hop_recv.at[i, distance - 1], along(-1)
                ).wait_recv()
            if distance < REACH:
                send(
                    remote(
                        half, window.at[i, at - 1, :, core], hop_send.at[i, distance], hop_recv.at[i, distance],
                        along(1),
                    )
                )
            send(remote(half, half, pair_send.at[i, distance], pair_recv.at[i, distance], pair))

    def key_tile(i, at, tile):
        return window[i, at, tile * PARTS : (tile + 1) * PARTS].reshape(BLOCK, HEAD)

    def tile_lanes(tile):
        return slice(tile * BLOCK, (tile + 1) * BLOCK)

    def forward(distance):
        at = REACH - distance
        for i in range(2):
            half = window.at[i, at, :, 1 - core]
            remote(half, half, pair_send.at[i, distance], pair_recv.at[i, distance], pair).wait_recv()
        for tile in range(BLOCKS):
            chunk_t[:, tile_lanes(tile)] = key_tile(1, at, tile).T
        key_at = lax.broadcasted_iota(jnp.int32, (BLOCK, BLOCK), 0)
        for block in range(BLOCKS):
            rows = block_rows(block)
            tiles = tiles_of(distance, block)

            @pl.loop(0, HEADS // 2)
            def _(two):
                for n in range(2):
                    head = two * 2 + n
                    best = None
                    for tile, slot in tiles:
                        one = dot(key_tile(0, at, tile), queries_t[head, :, rows])
                        first = at * STEP_ROWS + tile * BLOCK
                        allowed = key_at >= starts[:, rows] - first
                        if distance == 0 and tile == block:
                            allowed &= key_at <= lax.broadcasted_iota(jnp.int32, (1, BLOCK), 1)
                        one = jnp.where(allowed, one, NEGATIVE_FILL)
                        scores[n, tile] = one
                        one = jnp.max(one.reshape(BLOCK // 8, 8, BLOCK), axis=0)
                        best = one if best is None else jnp.maximum(best, one)
                    tops[n] = best
                for n in range(2):
                    head = two * 2 + n
                    old = top[head, :, rows]
                    new = jnp.maximum(old, jnp.max(tops[n], axis=0, keepdims=True))
                    fade = jnp.exp2((old - new) * SCALE_LOG2)
                    top[head, :, rows] = new
                    if distance < REACH:
                        chunk_tops[distance][head, :, rows] = new
                    summed, out = None, None
                    for tile, slot in tiles:
                        kept = jnp.exp2((scores[n, tile] - new) * SCALE_LOG2)
                        low = kept.astype(jnp.bfloat16)
                        probs[block * TILES + slot, head] = low
                        part = jnp.sum(kept.reshape(BLOCK // 8, 8, BLOCK), axis=0)
                        summed = part if summed is None else summed + part
                        part = dot(chunk_t[:, tile_lanes(tile)], low)
                        out = part if out is None else out + part
                    total[head, :, rows] = total[head, :, rows] * fade + jnp.sum(
                        summed, axis=0, keepdims=True
                    )
                    acc[head, :, rows] = acc[head, :, rows] * fade + out


    chunk_tops = [row_dot.at[1 + d] for d in range(REACH)]
    pass_on(0)
    send_rows(1, grads, grad_rows)
    pass_on(1)
    await_rows(0, query_rows)
    for head in range(HEADS):
        for block in range(BLOCKS):
            rows = block_rows(block)
            queries_t[head, :, rows] = query_rows[rows, head * HEAD : (head + 1) * HEAD].T
    for distance in range(REACH + 1):
        if distance >= 1 and distance < REACH:
            pass_on(distance + 1)
        forward(distance)
    await_rows(1, grad_rows)

    for head in range(HEADS):
        columns = slice(head * HEAD, (head + 1) * HEAD)
        for block in range(BLOCKS):
            rows = block_rows(block)
            row_total = total[head, :, rows]
            out_t = (acc[head, :, rows] / row_total).astype(jnp.bfloat16)
            out_rows[0, rows, columns] = out_t.T
            grad_t = grad_rows[rows, columns].T
            grads_t[head, :, rows] = grad_t
            row_dot[0, head, :, rows] = jnp.sum(
                grad_t.astype(jnp.float32) * out_t.astype(jnp.float32), axis=0, keepdims=True
            )
            total[head, :, rows] = top[head, :, rows] * SCALE_LOG2 + jnp.log2(row_total)
    acc[...] = jnp.zeros_like(acc)


    def out_copy(i, target, by):
        peer, device = ring(by)
        return remote(
            out_rows.at[i, token_rows(peer), :], target.at[:, row_columns(me)],
            out_send.at[i, by], out_recv.at[i, by], device,
        )

    def own_out(i, target):
        return pltpu.make_async_copy(
            out_rows.at[i, token_rows(me), :], target.at[:, row_columns(me)], out_own.at[i]
        )

    for by in range(1, RING):
        send(out_copy(0, attended, by))
    own_out(0, attended).start()

    def backward(distance, block):
        at = REACH - distance
        rows = block_rows(block)

        @pl.loop(0, HEADS // 2)
        def _(two):
            for tile, slot in tiles_of(distance, block):
                parts = slice(tile * PARTS, (tile + 1) * PARTS)
                key_sum = chunk_sums[0, parts].reshape(BLOCK, HEAD)
                value_sum = chunk_sums[1, parts].reshape(BLOCK, HEAD)
                for n in range(2):
                    head = two * 2 + n
                    then = top if distance == REACH else chunk_tops[distance]
                    factor = jnp.exp2(then[head, :, rows] * SCALE_LOG2 - total[head, :, rows])
                    probability = probs[block * TILES + slot, head].astype(jnp.float32) * factor
                    grad_probs = dot(key_tile(1, at, tile), grads_t[head, :, rows])
                    dscore = (probability * (grad_probs - row_dot[0, head, :, rows])).astype(jnp.bfloat16)
                    value_sum = value_sum + dot(
                        probability.astype(jnp.bfloat16), grad_rows[rows, head_columns(head)]
                    )
                    key_sum = key_sum + dot(dscore, query_rows[rows, head_columns(head)])
                    acc[head, :, rows] += dot(chunk_t[:, tile_lanes(tile)], dscore)
                chunk_sums[0, parts] = key_sum.reshape(PARTS, CORES, TOKENS, HEAD)
                chunk_sums[1, parts] = value_sum.reshape(PARTS, CORES, TOKENS, HEAD)

    def swap(distance):
        for i, scale in enumerate((SCALE, 1.0)):
            pair_out[distance, i] = (chunk_sums[i, :, 1 - core] * scale).astype(jnp.bfloat16)
            kept_sums[distance % 2, i] = chunk_sums[i, :, core] * scale
            send(
                remote(
                    pair_out.at[distance, i], pair_in.at[distance, i],
                    swap_send.at[distance, i], swap_recv.at[distance, i], pair,
                )
            )

    def combine(distance):
        for i, target in enumerate((key_grad, value_grad)):
            here = pair_in.at[distance, i]
            remote(here, here, swap_send.at[distance, i], swap_recv.at[distance, i], pair).wait_recv()
            summed = kept_sums[distance % 2, i] + pair_in[distance, i].astype(jnp.float32)
            if distance < REACH:
                here = hop_in.at[distance, i]
                remote(here, here, back_send.at[distance, i], back_recv.at[distance, i], along(1)).wait_recv()
                summed = summed + hop_in[distance, i].astype(jnp.float32)
            outgoing[distance, i] = summed.astype(jnp.bfloat16)
            if distance > 0:
                send(
                    remote(
                        outgoing.at[distance, i], hop_in.at[distance - 1, i],
                        back_send.at[distance - 1, i], back_recv.at[distance - 1, i], along(-1),
                    )
                )
                continue
            for by in range(1, X_SIZE):
                peer, device = across(by)
                send(
                    remote(
                        outgoing.at[0, i, peer], target.at[:, head_columns(x)],
                        sum_send.at[i, by], sum_recv.at[i, by], device,
                    )
                )
            pltpu.make_async_copy(outgoing.at[0, i, x], target.at[:, head_columns(x)], sum_own.at[i]).start()

    for distance in range(REACH, -1, -1):
        at = REACH - distance
        for tile in range(BLOCKS):
            chunk_t[:, tile_lanes(tile)] = key_tile(0, at, tile).T
        chunk_sums[...] = jnp.zeros_like(chunk_sums)
        backward(distance, 0)
        if distance < REACH:
            combine(distance + 1)
        backward(distance, 1)
        swap(distance)
    for head in range(HEADS):
        for block in range(BLOCKS):
            rows = block_rows(block)
            out_rows[1, rows, head * HEAD : (head + 1) * HEAD] = (
                (acc[head, :, rows] * SCALE).T.astype(jnp.bfloat16)
            )
    for by in range(1, RING):
        send(out_copy(1, query_grad, by))
    own_out(1, query_grad).start()
    combine(0)

    for i, target in enumerate((attended, query_grad)):
        own_out(i, target).wait()
        for by in range(1, RING):
            peer, device = ring(-by)
            here = target.at[:, row_columns(peer)]
            remote(here, here, out_send.at[i, by], out_recv.at[i, by], device).wait_recv()
    for i, target in enumerate((key_grad, value_grad)):
        pltpu.make_async_copy(outgoing.at[0, i, x], target.at[:, head_columns(x)], sum_own.at[i]).wait()
        for by in range(1, X_SIZE):
            peer, device = across(-by)
            here = target.at[:, head_columns(peer)]
            remote(here, here, sum_send.at[i, by], sum_recv.at[i, by], device).wait_recv()
    for copy in pending:
        copy.wait_send()


def shards(queries, keys, values, output_gradient, lengths):
    wide = jax.ShapeDtypeStruct((TOKENS, RING * WIDTH), jnp.bfloat16)
    narrow = jax.ShapeDtypeStruct((TOKENS, KEY_VALUE_HEADS * HEAD), jnp.bfloat16)
    dma = pltpu.SemaphoreType.DMA
    half = (X_SIZE, TOKENS, HEAD)
    low, full = jnp.bfloat16, jnp.float32
    pairs = HEADS * BLOCKS * TILES * BLOCK * BLOCK
    return pl.pallas_call(
        kernel,
        out_shape=(wide, wide, narrow, narrow),
        in_specs=[SMEM] + [ANY] * 4,
        out_specs=(ANY,) * 4,
        scratch_shapes=[
            pltpu.VMEM((2, REACH + 1, X_SIZE, CORES, TOKENS, HEAD), low),
            pltpu.VMEM((STEP_ROWS, WIDTH), low),
            pltpu.VMEM((STEP_ROWS, WIDTH), low),
            pltpu.VMEM((HEADS, HEAD, STEP_ROWS), low),
            pltpu.VMEM((HEADS, HEAD, STEP_ROWS), low),
            pltpu.VMEM((HEAD, STEP_ROWS), low),
            pltpu.VMEM((1, STEP_ROWS), jnp.int32),
            pltpu.VMEM((2, BLOCKS, BLOCK, BLOCK), full),
            pltpu.VMEM((BLOCKS * TILES, HEADS, BLOCK, BLOCK), low),
            pltpu.VMEM((2, 8, BLOCK), full),
            pltpu.VMEM((HEADS, 1, STEP_ROWS), full),
            pltpu.VMEM((HEADS, 1, STEP_ROWS), full),
            pltpu.VMEM((1 + REACH, HEADS, 1, STEP_ROWS), full),
            pltpu.VMEM((HEADS, HEAD, STEP_ROWS), full),
            pltpu.VMEM((2, STEP_ROWS, WIDTH), low),
            pltpu.VMEM((2, X_SIZE, CORES, TOKENS, HEAD), full),
            pltpu.VMEM((2, 2) + half, full),
            pltpu.VMEM((REACH + 1, 2) + half, low),
            pltpu.VMEM((REACH + 1, 2) + half, low),
            pltpu.VMEM((REACH, 2) + half, low),
            pltpu.VMEM((REACH + 1, 2) + half, low),
            dma((4,)), dma((2, RING)), dma((2, RING)), dma((2, X_SIZE)), dma((2, X_SIZE)),
            dma((2, REACH)), dma((2, REACH)), dma((2, REACH + 1)), dma((2, REACH + 1)),
            dma((2,)), dma((2, RING)), dma((2, RING)), dma((2,)), dma((2, X_SIZE)), dma((2, X_SIZE)),
            dma((REACH, 2)), dma((REACH, 2)), dma((REACH + 1, 2)), dma((REACH + 1, 2)),
        ],
        compiler_params=pltpu.CompilerParams(
            collective_id=0, has_side_effects=True, vmem_limit_bytes=64 * 2**20 - 2**16
        ),
        cost_estimate=pl.CostEstimate(
            flops=12 * HEAD * pairs, bytes_accessed=10 * 2**20, transcendentals=pairs
        ),
        name="attention",
    )(lengths, queries, output_gradient, keys, values)


def solution(mesh):
    wide = Mesh(
        mesh.devices.reshape(-1, Z_LOW, X_SIZE, CORES),
        ("blk", "zl", "x", "core"),
    )
    spec = P(("blk", "zl", "x", "core"), None)
    return jax.shard_map(
        shards,
        mesh=wide,
        in_specs=(spec, spec, spec, spec, P()),
        out_specs=(spec, spec, spec, spec),
        check_vma=False,
    )
```

```python
import math

import jax
import jax.numpy as jnp
from jax import lax
from jax.experimental import pallas as pl
from jax.experimental.pallas import tpu as pltpu
from jax.sharding import Mesh, PartitionSpec as P

HEAD = 128
KEY_VALUE_HEADS = 4

SCALE = 1.0 / math.sqrt(HEAD)
SCALE_LOG2 = SCALE * math.log2(math.e)
NEGATIVE_FILL = -1e30

Z_LOW, X_SIZE, CORES = 4, 4, 2
RING = X_SIZE * CORES
REACH = 4
TOKENS = 128
STEP_ROWS = TOKENS * RING
HEADS = 4
WIDTH = HEADS * HEAD

BLOCK = 512
BLOCKS = STEP_ROWS // BLOCK
PARTS = BLOCK // (CORES * TOKENS)
TILES = BLOCKS * REACH + 1

MESH = pl.DeviceIdType.MESH
ANY = pl.BlockSpec(memory_space=pl.ANY)
SMEM = pl.BlockSpec(memory_space=pltpu.SMEM)


def dot(a, b):
    return jnp.dot(a, b, preferred_element_type=jnp.float32)


def place():
    blk, zl = lax.axis_index("blk"), lax.axis_index("zl")
    x, core = lax.axis_index("x"), lax.axis_index("core")
    steps = lax.axis_size("blk") * Z_LOW

    def ring(by):
        peer = (x * CORES + core + by + RING) % RING
        return peer, (blk, zl, peer // CORES, peer % CORES)

    def along(by):
        step = (blk * Z_LOW + zl + by + steps) % steps
        return (step // Z_LOW, step % Z_LOW, x, core)

    def across(by):
        peer = (x + by + X_SIZE) % X_SIZE
        return peer, (blk, zl, peer, core)

    return blk * Z_LOW + zl, x * CORES + core, x, core, ring, along, across


def remote(src, dst, send, recv, device):
    return pltpu.make_async_remote_copy(
        src_ref=src, dst_ref=dst, send_sem=send, recv_sem=recv, device_id=device, device_id_type=MESH
    )


def head_columns(head):
    return pl.ds(pl.multiple_of(head * HEAD, HEAD), HEAD)


def row_columns(peer):
    return pl.ds(pl.multiple_of(peer * WIDTH, WIDTH), WIDTH)


def token_rows(peer):
    return pl.ds(pl.multiple_of(peer * TOKENS, TOKENS), TOKENS)


def block_rows(block):
    return slice(block * BLOCK, (block + 1) * BLOCK)


def tiles_of(distance, block):
    if distance == 0:
        return [(tile, tile) for tile in range(block + 1)]
    base = block + 1 + (distance - 1) * BLOCKS
    if distance == REACH:
        return [(tile, base + tile - block) for tile in range(block, BLOCKS)]
    return [(tile, base + tile) for tile in range(BLOCKS)]


def kernel(
    lengths, queries, grads, keys, values,
    attended, query_grad, key_grad, value_grad,
    window, query_rows, grad_rows, queries_t, grads_t, chunk_t, starts, scores, probs, tops, top, total, row_dot,
    acc, out_rows, chunk_sums, kept_sums, pair_out, pair_in, hop_in,
    own_sem, row_send, row_recv, head_send, head_recv, hop_send, hop_recv, pair_send, pair_recv,
    out_own, out_send, out_recv, sum_own, sum_send, sum_recv, back_send, back_recv, swap_send, swap_recv,
):
    step, me, x, core, ring, along, across = place()
    _, pair = ring(1 - 2 * core)

    barrier = pltpu.get_barrier_semaphore()
    for by in range(1, RING):
        pl.semaphore_signal(barrier, inc=1, device_id=ring(by)[1], device_id_type=MESH)
    for by in (1, -1):
        pl.semaphore_signal(barrier, inc=1, device_id=along(by), device_id_type=MESH)
    pl.semaphore_wait(barrier, RING + 1)

    pending = []

    def send(copy):
        copy.start()
        pending.append(copy)

    for i, source in enumerate((keys, values)):
        for by in range(1, X_SIZE):
            peer, device = across(by)
            send(
                remote(
                    source.at[:, head_columns(peer)], window.at[i, REACH, x, core],
                    head_send.at[i, by], head_recv.at[i, by], device,
                )
            )
    own = [
        pltpu.make_async_copy(source.at[:, head_columns(x)], window.at[i, REACH, x, core], own_sem.at[i])
        for i, source in enumerate((keys, values))
    ]
    row_parts = (
        (queries, query_rows, 0, WIDTH // 2),
        (queries, query_rows, WIDTH // 2, WIDTH // 2),
        (grads, grad_rows, 0, WIDTH),
    )

    def from_owner(i, peer):
        source, _, first, width = row_parts[i]
        return source.at[:, pl.ds(pl.multiple_of(peer * WIDTH + first, HEAD), width)]

    def at_holder(i, peer):
        _, target, first, width = row_parts[i]
        return target.at[token_rows(peer), pl.ds(first, width)]

    own += [
        pltpu.make_async_copy(from_owner(i, me), at_holder(i, me), own_sem.at[2 + i]) for i in range(3)
    ]
    for copy in own:
        copy.start()

    def send_rows(i):
        for by in range(1, RING):
            peer, device = ring(by)
            send(
                remote(
                    from_owner(i, peer), at_holder(i, me), row_send.at[i, by], row_recv.at[i, by], device
                )
            )

    def await_rows(i):
        own[2 + i].wait()
        for by in range(1, RING):
            peer, device = ring(-by)
            here = at_holder(i, peer)
            remote(here, here, row_send.at[i, by], row_recv.at[i, by], device).wait_recv()

    send_rows(0)
    send_rows(1)

    base = (step - REACH) * STEP_ROWS
    places = REACH * STEP_ROWS + lax.broadcasted_iota(jnp.int32, (1, STEP_ROWS), 1)

    def next_document(i, carried):
        end, row = carried
        end = end + lengths[i]
        return end, jnp.where(end <= places, end, row)

    _, row = lax.fori_loop(
        0, lengths.shape[0], next_document, (-base, jnp.zeros((1, STEP_ROWS), jnp.int32) - base)
    )
    starts[...] = row
    top[...] = jnp.full_like(top, NEGATIVE_FILL)
    total[...] = jnp.zeros_like(total)
    acc[...] = jnp.zeros_like(acc)

    def pass_on(distance):
        at = REACH - distance
        for i in range(2):
            half = window.at[i, at, :, core]
            if distance == 0:
                own[i].wait()
                for by in range(1, X_SIZE):
                    peer, device = across(-by)
                    here = window.at[i, REACH, peer, core]
                    remote(here, here, head_send.at[i, by], head_recv.at[i, by], device).wait_recv()
            else:
                remote(
                    half, half, hop_send.at[i, distance - 1], hop_recv.at[i, distance - 1], along(-1)
                ).wait_recv()
            if distance < REACH:
                send(
                    remote(
                        half, window.at[i, at - 1, :, core], hop_send.at[i, distance], hop_recv.at[i, distance],
                        along(1),
                    )
                )
            send(remote(half, half, pair_send.at[i, distance], pair_recv.at[i, distance], pair))

    def key_tile(i, at, tile):
        return window[i, at, tile * PARTS : (tile + 1) * PARTS].reshape(BLOCK, HEAD)

    def tile_lanes(tile):
        return slice(tile * BLOCK, (tile + 1) * BLOCK)

    def take(distance):
        at = REACH - distance
        for i in range(2):
            half = window.at[i, at, :, 1 - core]
            remote(half, half, pair_send.at[i, distance], pair_recv.at[i, distance], pair).wait_recv()
        for tile in range(BLOCKS):
            chunk_t[0, :, tile_lanes(tile)] = key_tile(1, at, tile).T

    def forward(distance, first_two=0, last_two=HEADS // 2):
        at = REACH - distance
        key_at = lax.broadcasted_iota(jnp.int32, (BLOCK, BLOCK), 0)
        for block in range(BLOCKS):
            rows = block_rows(block)
            tiles = tiles_of(distance, block)

            @pl.loop(first_two, last_two)
            def _(two):
                for n in range(2):
                    head = two * 2 + n
                    best = None
                    for tile, slot in tiles:
                        one = dot(key_tile(0, at, tile), queries_t[head, :, rows])
                        first = at * STEP_ROWS + tile * BLOCK
                        allowed = key_at >= starts[:, rows] - first
                        if distance == 0 and tile == block:
                            allowed &= key_at <= lax.broadcasted_iota(jnp.int32, (1, BLOCK), 1)
                        one = jnp.where(allowed, one, NEGATIVE_FILL)
                        scores[n, tile] = one
                        one = jnp.max(one.reshape(BLOCK // 8, 8, BLOCK), axis=0)
                        best = one if best is None else jnp.maximum(best, one)
                    tops[n] = best
                for n in range(2):
                    head = two * 2 + n
                    old = top[head, :, rows]
                    new = jnp.maximum(old, jnp.max(tops[n], axis=0, keepdims=True))
                    fade = jnp.exp2((old - new) * SCALE_LOG2)
                    top[head, :, rows] = new
                    if distance < REACH:
                        chunk_tops[distance][head, :, rows] = new
                    summed, out = None, None
                    for tile, slot in tiles:
                        kept = jnp.exp2((scores[n, tile] - new) * SCALE_LOG2)
                        low = kept.astype(jnp.bfloat16)
                        probs[block * TILES + slot, head] = low
                        part = jnp.sum(kept.reshape(BLOCK // 8, 8, BLOCK), axis=0)
                        summed = part if summed is None else summed + part
                        part = dot(chunk_t[0, :, tile_lanes(tile)], low)
                        out = part if out is None else out + part
                    total[head, :, rows] = total[head, :, rows] * fade + jnp.sum(
                        summed, axis=0, keepdims=True
                    )
                    acc[head, :, rows] = acc[head, :, rows] * fade + out


    chunk_tops = [row_dot.at[1 + d] for d in range(REACH)]
    pass_on(0)
    pass_on(1)
    take(0)
    for half in range(2):
        await_rows(half)
        if half == 1:
            send_rows(2)
        for head in range(half * HEADS // 2, (half + 1) * HEADS // 2):
            for block in range(BLOCKS):
                rows = block_rows(block)
                queries_t[head, :, rows] = query_rows[rows, head * HEAD : (head + 1) * HEAD].T
        forward(0, half * HEADS // 4, (half + 1) * HEADS // 4)
    for distance in range(1, REACH + 1):
        if distance < REACH:
            pass_on(distance + 1)
        take(distance)
        forward(distance)
    await_rows(2)

    for head in range(HEADS):
        columns = slice(head * HEAD, (head + 1) * HEAD)
        for block in range(BLOCKS):
            rows = block_rows(block)
            row_total = total[head, :, rows]
            out_t = (acc[head, :, rows] / row_total).astype(jnp.bfloat16)
            out_rows[0, rows, columns] = out_t.T
            grad_t = grad_rows[rows, columns].T
            grads_t[head, :, rows] = grad_t
            row_dot[0, head, :, rows] = jnp.sum(
                grad_t.astype(jnp.float32) * out_t.astype(jnp.float32), axis=0, keepdims=True
            )
            total[head, :, rows] = top[head, :, rows] * SCALE_LOG2 + jnp.log2(row_total)
    acc[...] = jnp.zeros_like(acc)


    def out_copy(i, target, by):
        peer, device = ring(by)
        return remote(
            out_rows.at[i, token_rows(peer), :], target.at[:, row_columns(me)],
            out_send.at[i, by], out_recv.at[i, by], device,
        )

    def own_out(i, target):
        return pltpu.make_async_copy(
            out_rows.at[i, token_rows(me), :], target.at[:, row_columns(me)], out_own.at[i]
        )

    for by in range(1, RING):
        send(out_copy(0, attended, by))
    own_out(0, attended).start()

    def backward(distance, block):
        at = REACH - distance
        rows = block_rows(block)
        sums = chunk_sums.at[0]

        @pl.loop(0, HEADS // 2)
        def _(two):
            for tile, slot in tiles_of(distance, block):
                parts = slice(tile * PARTS, (tile + 1) * PARTS)
                key_sum = sums[0, parts].reshape(BLOCK, HEAD)
                value_sum = sums[1, parts].reshape(BLOCK, HEAD)
                for n in range(2):
                    head = two * 2 + n
                    then = top if distance == REACH else chunk_tops[distance]
                    factor = jnp.exp2(then[head, :, rows] * SCALE_LOG2 - total[head, :, rows])
                    probability = probs[block * TILES + slot, head].astype(jnp.float32) * factor
                    grad_probs = dot(key_tile(1, at, tile), grads_t[head, :, rows])
                    dscore = (probability * (grad_probs - row_dot[0, head, :, rows])).astype(jnp.bfloat16)
                    value_sum = value_sum + dot(
                        probability.astype(jnp.bfloat16), grad_rows[rows, head_columns(head)]
                    )
                    key_sum = key_sum + dot(dscore, query_rows[rows, head_columns(head)])
                    acc[head, :, rows] += dot(chunk_t[0, :, tile_lanes(tile)], dscore)
                sums[0, parts] = key_sum.reshape(PARTS, CORES, TOKENS, HEAD)
                sums[1, parts] = value_sum.reshape(PARTS, CORES, TOKENS, HEAD)

    def swap(distance):
        sums = chunk_sums.at[0]
        for i, scale in enumerate((SCALE, 1.0)):
            pair_out[distance, i] = (sums[i, :, 1 - core] * scale).astype(jnp.bfloat16)
            kept_sums[distance % 2, i] = sums[i, :, core] * scale
            swap_copy(distance, i).start()

    def swap_copy(distance, i):
        return remote(
            pair_out.at[distance, i], pair_in.at[distance, i],
            swap_send.at[distance, i], swap_recv.at[distance, i], pair,
        )

    def combine(distance):
        for i, target in enumerate((key_grad, value_grad)):
            swap_copy(distance, i).wait()
            summed = kept_sums[distance % 2, i] + pair_in[distance, i].astype(jnp.float32)
            if distance < REACH:
                here = hop_in.at[distance, i]
                remote(here, here, back_send.at[distance, i], back_recv.at[distance, i], along(1)).wait_recv()
                summed = summed + hop_in[distance, i].astype(jnp.float32)
            pair_out[distance, i] = summed.astype(jnp.bfloat16)
            if distance > 0:
                send(
                    remote(
                        pair_out.at[distance, i], hop_in.at[distance - 1, i],
                        back_send.at[distance - 1, i], back_recv.at[distance - 1, i], along(-1),
                    )
                )
                continue
            for by in range(1, X_SIZE):
                peer, device = across(by)
                send(
                    remote(
                        pair_out.at[0, i, peer], target.at[:, head_columns(x)],
                        sum_send.at[i, by], sum_recv.at[i, by], device,
                    )
                )
            pltpu.make_async_copy(pair_out.at[0, i, x], target.at[:, head_columns(x)], sum_own.at[i]).start()

    def finish(block):
        rows = block_rows(block)
        for head in range(HEADS):
            out_rows[1, rows, head * HEAD : (head + 1) * HEAD] = (
                (acc[head, :, rows] * SCALE).T.astype(jnp.bfloat16)
            )
        for by in range(1, RING):
            peer, _ = ring(by)

            @pl.when(peer // (RING // BLOCKS) == block)
            def _():
                out_copy(1, query_grad, by).start()

        @pl.when(me // (RING // BLOCKS) == block)
        def _():
            own_out(1, query_grad).start()

    for distance in range(REACH, -1, -1):
        for tile in range(BLOCKS):
            chunk_t[0, :, tile_lanes(tile)] = key_tile(0, REACH - distance, tile).T
        chunk_sums[...] = jnp.zeros_like(chunk_sums)
        backward(distance, 0)
        if distance == 0:
            finish(0)
        if distance < REACH:
            combine(distance + 1)
        backward(distance, 1)
        swap(distance)
    finish(1)
    for by in range(1, RING):
        pending.append(out_copy(1, query_grad, by))
    combine(0)

    for i, target in enumerate((attended, query_grad)):
        own_out(i, target).wait()
        for by in range(1, RING):
            peer, device = ring(-by)
            here = target.at[:, row_columns(peer)]
            remote(here, here, out_send.at[i, by], out_recv.at[i, by], device).wait_recv()
    for i, target in enumerate((key_grad, value_grad)):
        pltpu.make_async_copy(pair_out.at[0, i, x], target.at[:, head_columns(x)], sum_own.at[i]).wait()
        for by in range(1, X_SIZE):
            peer, device = across(-by)
            here = target.at[:, head_columns(peer)]
            remote(here, here, sum_send.at[i, by], sum_recv.at[i, by], device).wait_recv()
    for copy in pending:
        copy.wait_send()


def shards(queries, keys, values, output_gradient, lengths):
    wide = jax.ShapeDtypeStruct((TOKENS, RING * WIDTH), jnp.bfloat16)
    narrow = jax.ShapeDtypeStruct((TOKENS, KEY_VALUE_HEADS * HEAD), jnp.bfloat16)
    dma = pltpu.SemaphoreType.DMA
    half = (X_SIZE, TOKENS, HEAD)
    low, full = jnp.bfloat16, jnp.float32
    pairs = HEADS * BLOCKS * TILES * BLOCK * BLOCK
    return pl.pallas_call(
        kernel,
        out_shape=(wide, wide, narrow, narrow),
        in_specs=[SMEM] + [ANY] * 4,
        out_specs=(ANY,) * 4,
        scratch_shapes=[
            pltpu.VMEM((2, REACH + 1, X_SIZE, CORES, TOKENS, HEAD), low),
            pltpu.VMEM((STEP_ROWS, WIDTH), low),
            pltpu.VMEM((STEP_ROWS, WIDTH), low),
            pltpu.VMEM((HEADS, HEAD, STEP_ROWS), low),
            pltpu.VMEM((HEADS, HEAD, STEP_ROWS), low),
            pltpu.VMEM((1, HEAD, STEP_ROWS), low),
            pltpu.VMEM((1, STEP_ROWS), jnp.int32),
            pltpu.VMEM((2, BLOCKS, BLOCK, BLOCK), full),
            pltpu.VMEM((BLOCKS * TILES, HEADS, BLOCK, BLOCK), low),
            pltpu.VMEM((2, 8, BLOCK), full),
            pltpu.VMEM((HEADS, 1, STEP_ROWS), full),
            pltpu.VMEM((HEADS, 1, STEP_ROWS), full),
            pltpu.VMEM((1 + REACH, HEADS, 1, STEP_ROWS), full),
            pltpu.VMEM((HEADS, HEAD, STEP_ROWS), full),
            pltpu.VMEM((2, STEP_ROWS, WIDTH), low),
            pltpu.VMEM((1, 2, X_SIZE, CORES, TOKENS, HEAD), full),
            pltpu.VMEM((2, 2) + half, full),
            pltpu.VMEM((REACH + 1, 2) + half, low),
            pltpu.VMEM((REACH + 1, 2) + half, low),
            pltpu.VMEM((REACH, 2) + half, low),
            dma((5,)), dma((3, RING)), dma((3, RING)), dma((2, X_SIZE)), dma((2, X_SIZE)),
            dma((2, REACH)), dma((2, REACH)), dma((2, REACH + 1)), dma((2, REACH + 1)),
            dma((2,)), dma((2, RING)), dma((2, RING)), dma((2,)), dma((2, X_SIZE)), dma((2, X_SIZE)),
            dma((REACH, 2)), dma((REACH, 2)), dma((REACH + 1, 2)), dma((REACH + 1, 2)),
        ],
        compiler_params=pltpu.CompilerParams(
            collective_id=0, has_side_effects=True, vmem_limit_bytes=64 * 2**20 - 2**16
        ),
        cost_estimate=pl.CostEstimate(
            flops=12 * HEAD * pairs, bytes_accessed=10 * 2**20, transcendentals=pairs
        ),
        name="attention",
    )(lengths, queries, output_gradient, keys, values)


def solution(mesh):
    wide = Mesh(
        mesh.devices.reshape(-1, Z_LOW, X_SIZE, CORES),
        ("blk", "zl", "x", "core"),
    )
    spec = P(("blk", "zl", "x", "core"), None)
    return jax.shard_map(
        shards,
        mesh=wide,
        in_specs=(spec, spec, spec, spec, P()),
        out_specs=(spec, spec, spec, spec),
        check_vma=False,
    )
```

```python
import math

import jax
import jax.numpy as jnp
from jax import lax
from jax.experimental import pallas as pl
from jax.experimental.pallas import tpu as pltpu
from jax.sharding import Mesh, PartitionSpec as P

HEAD = 128
KEY_VALUE_HEADS = 4

SCALE = 1.0 / math.sqrt(HEAD)
SCALE_LOG2 = SCALE * math.log2(math.e)
NEGATIVE_FILL = -1e30

Z_LOW, X_SIZE, CORES = 4, 4, 2
RING = X_SIZE * CORES
REACH = 4
TOKENS = 128
STEP_ROWS = TOKENS * RING
HEADS = 4
WIDTH = HEADS * HEAD

BLOCK = 512
BLOCKS = STEP_ROWS // BLOCK
PARTS = BLOCK // (CORES * TOKENS)
TILES = BLOCKS * REACH + 1

MESH = pl.DeviceIdType.MESH
ANY = pl.BlockSpec(memory_space=pl.ANY)
SMEM = pl.BlockSpec(memory_space=pltpu.SMEM)


def dot(a, b):
    return jnp.dot(a, b, preferred_element_type=jnp.float32)


def place():
    blk, zl = lax.axis_index("blk"), lax.axis_index("zl")
    x, core = lax.axis_index("x"), lax.axis_index("core")
    steps = lax.axis_size("blk") * Z_LOW

    def ring(by):
        peer = (x * CORES + core + by + RING) % RING
        return peer, (blk, zl, peer // CORES, peer % CORES)

    def along(by):
        step = (blk * Z_LOW + zl + by + steps) % steps
        return (step // Z_LOW, step % Z_LOW, x, core)

    def across(by):
        peer = (x + by + X_SIZE) % X_SIZE
        return peer, (blk, zl, peer, core)

    return blk * Z_LOW + zl, x * CORES + core, x, core, ring, along, across


def remote(src, dst, send, recv, device):
    return pltpu.make_async_remote_copy(
        src_ref=src, dst_ref=dst, send_sem=send, recv_sem=recv, device_id=device, device_id_type=MESH
    )


def head_columns(head):
    return pl.ds(pl.multiple_of(head * HEAD, HEAD), HEAD)


def row_columns(peer):
    return pl.ds(pl.multiple_of(peer * WIDTH, WIDTH), WIDTH)


def token_rows(peer):
    return pl.ds(pl.multiple_of(peer * TOKENS, TOKENS), TOKENS)


def block_rows(block):
    return slice(block * BLOCK, (block + 1) * BLOCK)


def tiles_of(distance, block):
    if distance == 0:
        return [(tile, tile) for tile in range(block + 1)]
    base = block + 1 + (distance - 1) * BLOCKS
    if distance == REACH:
        return [(tile, base + tile - block) for tile in range(block, BLOCKS)]
    return [(tile, base + tile) for tile in range(BLOCKS)]


HALF = BLOCK // 2


def pieces_of(distance, block, tile):
    whole, low, high = slice(0, BLOCK), slice(0, HALF), slice(HALF, BLOCK)
    if tile == block and distance == 0:
        return [(low, low), (high, whole)]
    if tile == block and distance == REACH:
        return [(low, whole), (high, high)]
    return [(whole, whole)]


def kernel(
    lengths, queries, grads, keys, values,
    attended, query_grad, key_grad, value_grad,
    window, query_rows, grad_rows, queries_t, grads_t, chunk_t, starts, scores, probs, tops, top, total, row_dot,
    acc, out_rows, chunk_sums, kept_sums, pair_out, pair_in, hop_in,
    own_sem, row_send, row_recv, head_send, head_recv, hop_send, hop_recv, pair_send, pair_recv,
    out_own, out_send, out_recv, sum_own, sum_send, sum_recv, back_send, back_recv, swap_send, swap_recv,
):
    step, me, x, core, ring, along, across = place()
    _, pair = ring(1 - 2 * core)

    barrier = pltpu.get_barrier_semaphore()
    for by in range(1, RING):
        pl.semaphore_signal(barrier, inc=1, device_id=ring(by)[1], device_id_type=MESH)
    for by in (1, -1):
        pl.semaphore_signal(barrier, inc=1, device_id=along(by), device_id_type=MESH)
    pl.semaphore_wait(barrier, RING + 1)

    pending = []

    def send(copy):
        copy.start()
        pending.append(copy)

    for i, source in enumerate((keys, values)):
        for by in range(1, X_SIZE):
            peer, device = across(by)
            send(
                remote(
                    source.at[:, head_columns(peer)], window.at[i, REACH, x, core],
                    head_send.at[i, by], head_recv.at[i, by], device,
                )
            )
    own = [
        pltpu.make_async_copy(source.at[:, head_columns(x)], window.at[i, REACH, x, core], own_sem.at[i])
        for i, source in enumerate((keys, values))
    ]
    row_parts = (
        (queries, query_rows, 0, WIDTH // 2),
        (queries, query_rows, WIDTH // 2, WIDTH // 2),
        (grads, grad_rows, 0, WIDTH),
    )

    def from_owner(i, peer):
        source, _, first, width = row_parts[i]
        return source.at[:, pl.ds(pl.multiple_of(peer * WIDTH + first, HEAD), width)]

    def at_holder(i, peer):
        _, target, first, width = row_parts[i]
        return target.at[token_rows(peer), pl.ds(first, width)]

    own += [
        pltpu.make_async_copy(from_owner(i, me), at_holder(i, me), own_sem.at[2 + i]) for i in range(3)
    ]
    for copy in own:
        copy.start()

    def send_rows(i):
        for by in range(1, RING):
            peer, device = ring(by)
            send(
                remote(
                    from_owner(i, peer), at_holder(i, me), row_send.at[i, by], row_recv.at[i, by], device
                )
            )

    def await_rows(i):
        own[2 + i].wait()
        for by in range(1, RING):
            peer, device = ring(-by)
            here = at_holder(i, peer)
            remote(here, here, row_send.at[i, by], row_recv.at[i, by], device).wait_recv()

    send_rows(0)
    send_rows(1)

    base = (step - REACH) * STEP_ROWS
    places = REACH * STEP_ROWS + lax.broadcasted_iota(jnp.int32, (1, STEP_ROWS), 1)

    def next_document(i, carried):
        end, row = carried
        end = end + lengths[i]
        return end, jnp.where(end <= places, end, row)

    _, row = lax.fori_loop(
        0, lengths.shape[0], next_document, (-base, jnp.zeros((1, STEP_ROWS), jnp.int32) - base)
    )
    starts[...] = row
    top[...] = jnp.full_like(top, NEGATIVE_FILL)
    total[...] = jnp.zeros_like(total)
    acc[...] = jnp.zeros_like(acc)

    def pass_on(distance):
        at = REACH - distance
        for i in range(2):
            half = window.at[i, at, :, core]
            if distance == 0:
                own[i].wait()
                for by in range(1, X_SIZE):
                    peer, device = across(-by)
                    here = window.at[i, REACH, peer, core]
                    remote(here, here, head_send.at[i, by], head_recv.at[i, by], device).wait_recv()
            else:
                remote(
                    half, half, hop_send.at[i, distance - 1], hop_recv.at[i, distance - 1], along(-1)
                ).wait_recv()
            if distance < REACH:
                send(
                    remote(
                        half, window.at[i, at - 1, :, core], hop_send.at[i, distance], hop_recv.at[i, distance],
                        along(1),
                    )
                )
            send(remote(half, half, pair_send.at[i, distance], pair_recv.at[i, distance], pair))

    def parts_of(tile, part):
        return slice((tile * BLOCK + part.start) // (CORES * TOKENS), (tile * BLOCK + part.stop) // (CORES * TOKENS))

    def key_tile(i, at, tile, part=slice(0, BLOCK)):
        return window[i, at, parts_of(tile, part)].reshape(part.stop - part.start, HEAD)

    def tile_lanes(tile, part=slice(0, BLOCK)):
        return slice(tile * BLOCK + part.start, tile * BLOCK + part.stop)

    def take(distance):
        at = REACH - distance
        for i in range(2):
            half = window.at[i, at, :, 1 - core]
            remote(half, half, pair_send.at[i, distance], pair_recv.at[i, distance], pair).wait_recv()
        for tile in range(BLOCKS):
            chunk_t[0, :, tile_lanes(tile)] = key_tile(1, at, tile).T

    def forward(distance, first_two=0, last_two=HEADS // 2):
        at = REACH - distance
        for block in range(BLOCKS):
            rows = block_rows(block)
            work = [
                (tile, slot, few, part)
                for tile, slot in tiles_of(distance, block)
                for few, part in pieces_of(distance, block, tile)
            ]
            work.sort(key=lambda one: one[2].stop - one[2].start, reverse=True)
            wide = [one for one in work if one[2].stop - one[2].start == BLOCK]

            @pl.loop(first_two, last_two)
            def _(two):
                for n in range(2):
                    head = two * 2 + n
                    best = {}
                    for tile, slot, few, part in work:
                        some = tile_lanes(block, few)
                        keys_here, queries_here = part.stop - part.start, few.stop - few.start
                        one = dot(key_tile(0, at, tile, part), queries_t[head, :, some])
                        key_at = lax.broadcasted_iota(jnp.int32, (keys_here, queries_here), 0)
                        allowed = key_at >= starts[:, some] - (at * STEP_ROWS + tile * BLOCK + part.start)
                        if distance == 0 and tile == block:
                            query_at = lax.broadcasted_iota(jnp.int32, (1, queries_here), 1)
                            allowed &= key_at <= query_at + (few.start - part.start)
                        one = jnp.where(allowed, one, NEGATIVE_FILL)
                        scores[n, tile, part, few] = one
                        one = jnp.max(one.reshape(keys_here // 8, 8, queries_here), axis=0)
                        if queries_here == BLOCK:
                            best[0] = jnp.maximum(best[0], one) if best else one
                            tops[n] = best[0]
                        else:
                            tops[n, :, few] = jnp.maximum(tops[n, :, few], one) if wide else one
                for n in range(2):
                    head = two * 2 + n
                    old = top[head, :, rows]
                    new = jnp.maximum(old, jnp.max(tops[n], axis=0, keepdims=True))
                    fade = jnp.exp2((old - new) * SCALE_LOG2)
                    top[head, :, rows] = new
                    if distance < REACH:
                        chunk_tops[distance][head, :, rows] = new
                    summed, out = None, None
                    for tile, slot, few, part in work:
                        some = tile_lanes(block, few)
                        keys_here, queries_here = part.stop - part.start, few.stop - few.start
                        kept = jnp.exp2((scores[n, tile, part, few] - new[:, few]) * SCALE_LOG2)
                        low = kept.astype(jnp.bfloat16)
                        probs[block * TILES + slot, head, part, few] = low
                        one = jnp.sum(kept.reshape(keys_here // 8, 8, queries_here), axis=0)
                        more = dot(chunk_t[0, :, tile_lanes(tile, part)], low)
                        if queries_here == BLOCK:
                            summed = one if summed is None else summed + one
                            out = more if out is None else out + more
                            if (tile, slot, few, part) != wide[-1]:
                                continue
                            total[head, :, rows] = total[head, :, rows] * fade + jnp.sum(
                                summed, axis=0, keepdims=True
                            )
                            acc[head, :, rows] = acc[head, :, rows] * fade + out
                        else:
                            old_part = 1.0 if wide else fade[:, few]
                            total[head, :, some] = total[head, :, some] * old_part + jnp.sum(
                                one, axis=0, keepdims=True
                            )
                            acc[head, :, some] = acc[head, :, some] * old_part + more

    chunk_tops = [row_dot.at[1 + d] for d in range(REACH)]
    pass_on(0)
    pass_on(1)
    take(0)
    for half in range(2):
        await_rows(half)
        if half == 1:
            send_rows(2)
        for head in range(half * HEADS // 2, (half + 1) * HEADS // 2):
            for block in range(BLOCKS):
                rows = block_rows(block)
                queries_t[head, :, rows] = query_rows[rows, head * HEAD : (head + 1) * HEAD].T
        forward(0, half * HEADS // 4, (half + 1) * HEADS // 4)
    for distance in range(1, REACH + 1):
        if distance < REACH:
            pass_on(distance + 1)
        take(distance)
        forward(distance)
    await_rows(2)

    for head in range(HEADS):
        columns = slice(head * HEAD, (head + 1) * HEAD)
        for block in range(BLOCKS):
            rows = block_rows(block)
            row_total = total[head, :, rows]
            out_t = (acc[head, :, rows] / row_total).astype(jnp.bfloat16)
            out_rows[0, rows, columns] = out_t.T
            grad_t = grad_rows[rows, columns].T
            grads_t[head, :, rows] = grad_t
            row_dot[0, head, :, rows] = jnp.sum(
                grad_t.astype(jnp.float32) * out_t.astype(jnp.float32), axis=0, keepdims=True
            )
            total[head, :, rows] = top[head, :, rows] * SCALE_LOG2 + jnp.log2(row_total)
    acc[...] = jnp.zeros_like(acc)


    def out_copy(i, target, by):
        peer, device = ring(by)
        return remote(
            out_rows.at[i, token_rows(peer), :], target.at[:, row_columns(me)],
            out_send.at[i, by], out_recv.at[i, by], device,
        )

    def own_out(i, target):
        return pltpu.make_async_copy(
            out_rows.at[i, token_rows(me), :], target.at[:, row_columns(me)], out_own.at[i]
        )

    for by in range(1, RING):
        send(out_copy(0, attended, by))
    own_out(0, attended).start()

    def backward(distance, block):
        at = REACH - distance
        rows = block_rows(block)
        sums = chunk_sums.at[0]

        @pl.loop(0, HEADS // 2)
        def _(two):
            for tile, slot in tiles_of(distance, block):
                for few, part in pieces_of(distance, block, tile):
                    some, parts = tile_lanes(block, few), parts_of(tile, part)
                    shape = (parts.stop - parts.start, CORES, TOKENS, HEAD)
                    key_sum = sums[0, parts].reshape(-1, HEAD)
                    value_sum = sums[1, parts].reshape(-1, HEAD)
                    for n in range(2):
                        head = two * 2 + n
                        then = top if distance == REACH else chunk_tops[distance]
                        factor = jnp.exp2(then[head, :, some] * SCALE_LOG2 - total[head, :, some])
                        probability = (
                            probs[block * TILES + slot, head, part, few].astype(jnp.float32) * factor
                        )
                        grad_probs = dot(key_tile(1, at, tile, part), grads_t[head, :, some])
                        dscore = (probability * (grad_probs - row_dot[0, head, :, some])).astype(jnp.bfloat16)
                        value_sum = value_sum + dot(
                            probability.astype(jnp.bfloat16), grad_rows[some, head_columns(head)]
                        )
                        key_sum = key_sum + dot(dscore, query_rows[some, head_columns(head)])
                        acc[head, :, some] += dot(chunk_t[0, :, tile_lanes(tile, part)], dscore)
                    sums[0, parts] = key_sum.reshape(shape)
                    sums[1, parts] = value_sum.reshape(shape)

    def swap(distance):
        sums = chunk_sums.at[0]
        for i, scale in enumerate((SCALE, 1.0)):
            pair_out[distance, i] = (sums[i, :, 1 - core] * scale).astype(jnp.bfloat16)
            kept_sums[distance % 2, i] = sums[i, :, core] * scale
            swap_copy(distance, i).start()

    def swap_copy(distance, i):
        return remote(
            pair_out.at[distance, i], pair_in.at[distance, i],
            swap_send.at[distance, i], swap_recv.at[distance, i], pair,
        )

    def combine(distance):
        for i, target in enumerate((key_grad, value_grad)):
            swap_copy(distance, i).wait()
            summed = kept_sums[distance % 2, i] + pair_in[distance, i].astype(jnp.float32)
            if distance < REACH:
                here = hop_in.at[distance, i]
                remote(here, here, back_send.at[distance, i], back_recv.at[distance, i], along(1)).wait_recv()
                summed = summed + hop_in[distance, i].astype(jnp.float32)
            pair_out[distance, i] = summed.astype(jnp.bfloat16)
            if distance > 0:
                send(
                    remote(
                        pair_out.at[distance, i], hop_in.at[distance - 1, i],
                        back_send.at[distance - 1, i], back_recv.at[distance - 1, i], along(-1),
                    )
                )
                continue
            for by in range(1, X_SIZE):
                peer, device = across(by)
                send(
                    remote(
                        pair_out.at[0, i, peer], target.at[:, head_columns(x)],
                        sum_send.at[i, by], sum_recv.at[i, by], device,
                    )
                )
            pltpu.make_async_copy(pair_out.at[0, i, x], target.at[:, head_columns(x)], sum_own.at[i]).start()

    def finish(block):
        rows = block_rows(block)
        for head in range(HEADS):
            out_rows[1, rows, head * HEAD : (head + 1) * HEAD] = (
                (acc[head, :, rows] * SCALE).T.astype(jnp.bfloat16)
            )
        for by in range(1, RING):
            peer, _ = ring(by)

            @pl.when(peer // (RING // BLOCKS) == block)
            def _():
                out_copy(1, query_grad, by).start()

        @pl.when(me // (RING // BLOCKS) == block)
        def _():
            own_out(1, query_grad).start()

    for distance in range(REACH, -1, -1):
        for tile in range(BLOCKS):
            chunk_t[0, :, tile_lanes(tile)] = key_tile(0, REACH - distance, tile).T
        chunk_sums[...] = jnp.zeros_like(chunk_sums)
        backward(distance, 0)
        if distance == 0:
            finish(0)
        if distance < REACH:
            combine(distance + 1)
        backward(distance, 1)
        swap(distance)
    finish(1)
    for by in range(1, RING):
        pending.append(out_copy(1, query_grad, by))
    combine(0)

    for i, target in enumerate((attended, query_grad)):
        own_out(i, target).wait()
        for by in range(1, RING):
            peer, device = ring(-by)
            here = target.at[:, row_columns(peer)]
            remote(here, here, out_send.at[i, by], out_recv.at[i, by], device).wait_recv()
    for i, target in enumerate((key_grad, value_grad)):
        pltpu.make_async_copy(pair_out.at[0, i, x], target.at[:, head_columns(x)], sum_own.at[i]).wait()
        for by in range(1, X_SIZE):
            peer, device = across(-by)
            here = target.at[:, head_columns(peer)]
            remote(here, here, sum_send.at[i, by], sum_recv.at[i, by], device).wait_recv()
    for copy in pending:
        copy.wait_send()


def shards(queries, keys, values, output_gradient, lengths):
    wide = jax.ShapeDtypeStruct((TOKENS, RING * WIDTH), jnp.bfloat16)
    narrow = jax.ShapeDtypeStruct((TOKENS, KEY_VALUE_HEADS * HEAD), jnp.bfloat16)
    dma = pltpu.SemaphoreType.DMA
    half = (X_SIZE, TOKENS, HEAD)
    low, full = jnp.bfloat16, jnp.float32
    pairs = HEADS * BLOCKS * TILES * BLOCK * BLOCK
    return pl.pallas_call(
        kernel,
        out_shape=(wide, wide, narrow, narrow),
        in_specs=[SMEM] + [ANY] * 4,
        out_specs=(ANY,) * 4,
        scratch_shapes=[
            pltpu.VMEM((2, REACH + 1, X_SIZE, CORES, TOKENS, HEAD), low),
            pltpu.VMEM((STEP_ROWS, WIDTH), low),
            pltpu.VMEM((STEP_ROWS, WIDTH), low),
            pltpu.VMEM((HEADS, HEAD, STEP_ROWS), low),
            pltpu.VMEM((HEADS, HEAD, STEP_ROWS), low),
            pltpu.VMEM((1, HEAD, STEP_ROWS), low),
            pltpu.VMEM((1, STEP_ROWS), jnp.int32),
            pltpu.VMEM((2, BLOCKS, BLOCK, BLOCK), full),
            pltpu.VMEM((BLOCKS * TILES, HEADS, BLOCK, BLOCK), low),
            pltpu.VMEM((2, 8, BLOCK), full),
            pltpu.VMEM((HEADS, 1, STEP_ROWS), full),
            pltpu.VMEM((HEADS, 1, STEP_ROWS), full),
            pltpu.VMEM((1 + REACH, HEADS, 1, STEP_ROWS), full),
            pltpu.VMEM((HEADS, HEAD, STEP_ROWS), full),
            pltpu.VMEM((2, STEP_ROWS, WIDTH), low),
            pltpu.VMEM((1, 2, X_SIZE, CORES, TOKENS, HEAD), full),
            pltpu.VMEM((2, 2) + half, full),
            pltpu.VMEM((REACH + 1, 2) + half, low),
            pltpu.VMEM((REACH + 1, 2) + half, low),
            pltpu.VMEM((REACH, 2) + half, low),
            dma((5,)), dma((3, RING)), dma((3, RING)), dma((2, X_SIZE)), dma((2, X_SIZE)),
            dma((2, REACH)), dma((2, REACH)), dma((2, REACH + 1)), dma((2, REACH + 1)),
            dma((2,)), dma((2, RING)), dma((2, RING)), dma((2,)), dma((2, X_SIZE)), dma((2, X_SIZE)),
            dma((REACH, 2)), dma((REACH, 2)), dma((REACH + 1, 2)), dma((REACH + 1, 2)),
        ],
        compiler_params=pltpu.CompilerParams(
            collective_id=0, has_side_effects=True, vmem_limit_bytes=64 * 2**20 - 2**16
        ),
        cost_estimate=pl.CostEstimate(
            flops=12 * HEAD * pairs, bytes_accessed=10 * 2**20, transcendentals=pairs
        ),
        name="attention",
    )(lengths, queries, output_gradient, keys, values)


def solution(mesh):
    wide = Mesh(
        mesh.devices.reshape(-1, Z_LOW, X_SIZE, CORES),
        ("blk", "zl", "x", "core"),
    )
    spec = P(("blk", "zl", "x", "core"), None)
    return jax.shard_map(
        shards,
        mesh=wide,
        in_specs=(spec, spec, spec, spec, P()),
        out_specs=(spec, spec, spec, spec),
        check_vma=False,
    )
```
